512 devices in a mesh: row: 32 (over y_lo, z), col: 16 (over x, y_hi, core).
Axes of the slice: x: 4, y: 8 (y_hi: 2, y_lo: 4; y = y_hi * 4 + y_lo), z: 8, core: 2. Of those that a mesh axis runs over, the one named last changes fastest.
Arguments:
- grad_out: bfloat16 [65536, 256], P(('row', 'col')), may hold values from -6 to 6
- relu_mask: int32 [65536, 256], P(('row', 'col')), may hold values 0 or 1
- features: bfloat16 [16, 4096, 256], P('col', 'row'), may hold values from -0.119628906 to 0.119628906
- weight: bfloat16 [256, 256], replicated, may hold values from -0.375 to 0.375
- tile_values: bfloat16 [32, 16, 144, 128, 128], P('row', 'col'), may hold values from 0.0049743652 to 0.049804688
- tile_lists: int32 [32, 16, 3, 144], P('row', 'col'), may hold values from 0 to 511, as said below
- tile_count: int32 [32, 16], P('row', 'col'), may hold values from 18 to 144, as said below
Outputs:
- grad_input: bfloat16 [16, 4096, 256], P('col', 'row')
- grad_weight: float32 [256, 256], replicated
The draws below stay inside these ranges and needn't reach their ends.
Inputs may be any that keep to these rules, and one draw needn't show every extreme that they name: `tile_lists`: for device (r, c) the first tile_count[r, c] entries name distinct tiles with block row in r * 16 to (r + 1) * 16 - 1 and block column in c * 32 to (c + 1) * 32 - 1; row 2 of each device's list holds each slot 0 to 143 once; entries past the count lie in the same ranges and are ignored. `tile_count`: some device holds exactly 144 live entries.
All inputs are finite; a program needn't handle non-finite values. No bound on the sum of `relu_mask` on one device may be relied on, other than what follows from the above.
Results may differ from the reference program's by a relative error of at most 0.0049.
Values may be sent and summed in bfloat16 or wider, within the bound.
A program may use at most 128 MiB of HBM per device.

```python
import jax
import jax.numpy as jnp
from jax import lax

D = 256
BLOCK = 128
BR = 16
TILE_CAP = 144
BC = 32
NB = 512
NODES = 65536
N_ROW = 32
N_COL = 16


def draw_tile_lists(key, part):
    key = jax.random.fold_in(key, 11)
    devices = N_ROW * N_COL
    keys = jax.random.split(key, 2 * devices)

    def one_list(device):
        places = jax.random.permutation(keys[2 * device], BR * BC)[:TILE_CAP].astype(jnp.int32)
        slot_ids = jax.random.permutation(keys[2 * device + 1], TILE_CAP).astype(jnp.int32)
        row_id = device // N_COL
        col_id = device % N_COL
        block_rows = row_id * BR + places // BC
        block_cols = col_id * BC + places % BC
        return jnp.stack([block_rows, block_cols, slot_ids])
    stacked = jax.vmap(one_list)(jnp.arange(devices, dtype=jnp.int32))
    return stacked.reshape(N_ROW, N_COL, 3, TILE_CAP).astype(jnp.int32)


def draw_tile_count(key, part):
    key = jax.random.fold_in(key, 23)
    low_count = max(1, TILE_CAP // 8)
    high_count = max(low_count, TILE_CAP // 2) + 1
    counts = jax.random.randint(key, (N_ROW * N_COL,), low_count, high_count, dtype=jnp.int32)
    chosen = jax.random.randint(jax.random.fold_in(key, 5), (), 0, N_ROW * N_COL, dtype=jnp.int32)
    counts = jnp.where(jnp.arange(N_ROW * N_COL, dtype=jnp.int32) == chosen, TILE_CAP, counts)
    return counts.reshape(N_ROW, N_COL).astype(jnp.int32)


def plant(result, stream_key, smallest, largest):
    longest = result.shape.index(max(result.shape))
    spots = []
    for shift in (0, 1):
        where = [jax.random.randint(jax.random.fold_in(stream_key, axis), (), 0, length) for axis, length in enumerate(result.shape)]
        where[longest] = (where[longest] + shift) % result.shape[longest]
        spots.append(tuple(where))
    return result.at[spots[0]].set(smallest).at[spots[1]].set(largest)


def level_of(own_key, dims, shards, low, largest):
    factor_of, own = 1.0, jax.random.fold_in(own_key, 6)
    for position, shards_of in shards:
        heights = jnp.exp(jax.random.uniform(jax.random.fold_in(own, position), (shards_of,), jnp.float32, low / len(shards), largest / len(shards)))
        factor_of = factor_of * jnp.repeat(heights, dims[position] // shards_of).reshape([-1 if axis == position else 1 for axis in range(len(dims))])
    return factor_of


def gaussian(key, shape, width, most, cuts=(), held_as=jnp.bfloat16):
    result = jax.random.normal(key, shape, jnp.float32) * width
    if len(cuts) > 0:
        result = level_of(key, shape, cuts, -0.22, 0.18) * result
    return jnp.clip(result, min=-most, max=most).astype(held_as)


def setup_inputs(seed: int = 0) -> dict:
    key_list = jax.random.split(jax.random.key(seed), 8)
    grad_out = gaussian(key_list[0], (NODES, D), 1.0, 6.0, ((0, 512),))
    relu_mask = plant((jax.random.randint(key_list[1], (NODES, D), 0, 2) < 1).astype(jnp.int32), jax.random.fold_in(key_list[1], 1), 0, 1)
    features = gaussian(key_list[2], (N_COL, BC * BLOCK, D), 0.02, 0.119628906, ((0, 16), (1, 32)))
    weight = gaussian(key_list[3], (D, D), D ** -0.5, 0.375)
    tile_values = jnp.clip(0.0049743652 + 0.044830322 * jax.random.uniform(key_list[4], (N_ROW, N_COL, TILE_CAP, BLOCK, BLOCK), jnp.float32) ** level_of(key_list[4], (N_ROW, N_COL, TILE_CAP, BLOCK, BLOCK), ((0, 32), (1, 16)), -0.2, 0.2), 0.0049743652, 0.049804688).astype(jnp.bfloat16)
    tile_lists = draw_tile_lists(jax.random.fold_in(key_list[7], 71), 0)
    tile_count = draw_tile_count(jax.random.fold_in(key_list[7], 71), 0)
    return dict(grad_out=grad_out, relu_mask=relu_mask, features=features, weight=weight, tile_values=tile_values, tile_lists=tile_lists, tile_count=tile_count)


def reference(grad_out, relu_mask, features, weight, tile_values, tile_lists, tile_count):
    dz = grad_out * relu_mask.astype(jnp.bfloat16)
    dz_blocks = dz.reshape(NB, BLOCK, D).astype(jnp.float32)
    slots = jnp.arange(TILE_CAP, dtype=jnp.int32)

    def one_device(agg, device):
        row_id = device // N_COL
        col_id = device % N_COL
        lists = tile_lists[row_id, col_id]
        values = tile_values[row_id, col_id]
        valid = (slots < tile_count[row_id, col_id]).astype(jnp.float32)
        tiles = values[lists[2]].astype(jnp.float32)
        blocks = dz_blocks[lists[0]]
        prods = jnp.einsum("tik,tid->tkd", tiles, blocks, precision=lax.Precision.HIGHEST)
        prods = prods * valid[:, None, None]
        return agg.at[lists[1]].add(prods), None

    agg, _ = lax.scan(one_device, jnp.zeros((NB, BLOCK, D), jnp.float32), jnp.arange(N_ROW * N_COL, dtype=jnp.int32))
    agg_b = agg.reshape(NODES, D).astype(jnp.bfloat16)
    inputs = features.reshape(NODES, D)
    grad_input = lax.dot_general(agg_b, weight, (((1,), (1,)), ((), ())), preferred_element_type=jnp.float32)
    grad_input = grad_input.astype(jnp.bfloat16).reshape(N_COL, BC * BLOCK, D)
    grad_weight = lax.dot_general(inputs, agg_b, (((0,), (0,)), ((), ())), preferred_element_type=jnp.float32)
    return grad_input, grad_weight
```

```python
import functools

import jax
import jax.numpy as jnp
from jax import lax
from jax.experimental import pallas as pl
from jax.experimental.pallas import tpu as pltpu
from jax.sharding import PartitionSpec as P

NZ, NYL, NX = 8, 4, 4
NG = 8
NY = 8
BLOCK, D = 128, 256
BR, BC, CAP = 16, 32, 144
PIECES = 2
HALF = D // 2
F32, BF16 = jnp.float32, jnp.bfloat16


def kernel(
    go, mask, feat, wgt, tiles, table, gi, gw,
    tiles_v, ag, dzall, w, part, zsend, zrecv, sums, ysend, yrecv,
    w1, r1, s1, r2, s2, r3, f1, f2,
    tile_sem, ag_ss, ag_rs, z_ss, z_rs, y_ss, y_rs, g_ss, g_rs,
):
    row, col = lax.axis_index("row"), lax.axis_index("col")
    ylo, z = row // NZ, row % NZ
    x, yh, core = col // 4, (col // 2) % 2, col % 2
    g = x * 2 + core
    y = yh * NYL + ylo

    def g_peer(q):
        return row, (q // 2) * 4 + yh * 2 + q % 2

    def y_peer(q):
        return (q % NYL) * NZ + z, x * 4 + (q // NYL) * 2 + core

    def z_peer(q):
        return ylo * NZ + q, col

    def remote(src, dst, ssem, rsem, to):
        return pltpu.make_async_remote_copy(
            src_ref=src, dst_ref=dst, send_sem=ssem, recv_sem=rsem,
            device_id=to, device_id_type=pl.DeviceIdType.MESH,
        )

    sent = []

    def start(src, dst, ssem, rsem, to):
        copy = remote(src, dst, ssem, rsem, to)
        copy.start()
        sent.append(copy)

    def arrived(dst, sem, frm):
        remote(dst, dst, sem, sem, frm).wait_recv()

    tile_copies = []
    for i in range(4):
        part_of = pl.ds(i * (CAP // 4), CAP // 4)
        copy = pltpu.make_async_copy(tiles.at[part_of], tiles_v.at[part_of], tile_sem.at[i])
        copy.start()
        tile_copies.append(copy)

    barrier = pltpu.get_barrier_semaphore()
    for o in range(1, 8):
        for to in (g_peer((g + o) % NG), y_peer((y + o) % NY), z_peer((z + o) % NZ)):
            pl.semaphore_signal(barrier, inc=1, device_id=to, device_id_type=pl.DeviceIdType.MESH)
    dz = go[...].astype(F32) * mask[...].astype(F32)
    ag[col] = dz.T.astype(BF16)
    tiles_v[CAP] = jnp.zeros((BLOCK, BLOCK), BF16)
    pl.semaphore_wait(barrier, 21)

    rows = D // PIECES

    def slot_of(xq, yq, cq):
        return xq * 4 + yq * 2 + cq

    def ag_send(slot, p, to_col, k):
        ref = ag.at[slot, pl.ds(p * rows, rows)]
        start(ref, ref, ag_ss.at[k, p], ag_rs.at[slot, p], (row, to_col))

    def ag_wait(slot, p, from_col):
        arrived(ag.at[slot, pl.ds(p * rows, rows)], ag_rs.at[slot, p], (row, from_col))

    xs = [(x + o) % NX for o in (1, 3, 2)]
    for p in range(PIECES):
        ag_send(col, p, slot_of(x, 1 - yh, core), 0)
    for p in range(PIECES):
        for k, xq in enumerate(xs):
            ag_send(col, p, slot_of(xq, yh, core), 1 + k)
    for p in range(PIECES):
        ag_send(col, p, slot_of(x, yh, 1 - core), 4)
    over = slot_of(x, 1 - yh, core)
    for p in range(PIECES):
        ag_wait(over, p, over)
        for k, xq in enumerate(xs):
            ag_send(over, p, slot_of(xq, yh, core), 5 + k)
        ag_send(over, p, slot_of(x, yh, 1 - core), 8)
    for p in range(PIECES):
        for k, xq in enumerate(xs):
            ag_wait(slot_of(xq, yh, core), p, slot_of(xq, yh, core))
            ag_send(slot_of(xq, yh, core), p, slot_of(x, yh, 1 - core), 9 + k)
    for p in range(PIECES):
        for k, xq in enumerate(xs):
            ag_wait(slot_of(xq, 1 - yh, core), p, slot_of(xq, yh, core))
            ag_send(slot_of(xq, 1 - yh, core), p, slot_of(x, yh, 1 - core), 12 + k)
    for xq in range(NX):
        for yq in range(2):
            for p in range(PIECES):
                ag_wait(slot_of(xq, yq, 1 - core), p, slot_of(x, yh, 1 - core))
    for i in range(BR):
        dzall[:, i * BLOCK:(i + 1) * BLOCK] = ag[i]
    for copy in tile_copies:
        copy.wait()

    def compute(zq):
        def pair(h, carry):
            for j in range(2):
                first = ((2 * h + j) * NZ + zq) * BR
                for i in range(BR):
                    w[i * BLOCK:(i + 1) * BLOCK, j * BLOCK:(j + 1) * BLOCK] = tiles_v[table[first + i]]
            res = jnp.dot(dzall[...], w[...], preferred_element_type=F32)
            part[zq, 2 * h] = res[:, :BLOCK]
            part[zq, 2 * h + 1] = res[:, BLOCK:]
            return carry

        lax.fori_loop(0, NYL // 2, pair, 0)

    ways = (z_peer((z + 1) % NZ), z_peer((z + NZ - 1) % NZ))
    order = [(ylo + 1 + k) % NYL for k in range(NYL)]
    compute((z + 4) % NZ)
    for s in range(4):
        if s:
            compute((z + 4 - s) % NZ)
            compute((z + 4 + s) % NZ)
        for k, yq in enumerate(order):
            for d in range(2):
                dest = (z + 4 - s) % NZ if d == 0 else (z + 4 + s) % NZ
                mine = pl.ds(d * HALF, HALF)
                if s == 0:
                    zsend[d, s, yq, mine] = part[dest, yq, mine].astype(BF16)
                    src, dst = zsend.at[d, s, yq, mine], zrecv.at[d, s, yq, mine]
                elif s == 1:
                    arrived(zrecv.at[d, 0, yq, mine], z_rs.at[d, 0, yq], ways[1 - d])
                    other = pl.ds((1 - d) * HALF, HALF)
                    got = part[dest, yq, mine] + zrecv[d, 0, yq, mine].astype(F32)
                    zsend[d, s, yq, mine] = got.astype(BF16)
                    zsend[d, s, yq, other] = part[dest, yq, other].astype(BF16)
                    src, dst = zsend.at[d, s, yq], zrecv.at[d, s, yq]
                else:
                    arrived(zrecv.at[d, s - 1, yq], z_rs.at[d, s - 1, yq], ways[1 - d])
                    got = part[dest, yq] + zrecv[d, s - 1, yq].astype(F32)
                    zsend[d, s, yq] = got.astype(BF16)
                    src, dst = zsend.at[d, s, yq], zrecv.at[d, s, yq]
                start(src, dst, z_ss.at[d, s, yq], z_rs.at[d, s, yq], ways[d])
    compute(z)
    for k, yq in enumerate(order):
        for d in range(2):
            arrived(zrecv.at[d, 3, yq], z_rs.at[d, 3, yq], ways[1 - d])
        total = part[z, yq] + zrecv[0, 3, yq].astype(F32) + zrecv[1, 3, yq].astype(F32)
        if k < 3:
            ysend[yq] = total.astype(BF16)
            start(ysend.at[yq], yrecv.at[ylo], y_ss.at[yq], y_rs.at[ylo], (yq * NZ + z, col))
        else:
            sums[...] = total
    agg = sums[...]
    for yq in order[:3]:
        arrived(yrecv.at[yq], y_rs.at[yq], (yq * NZ + z, col))
        agg = agg + yrecv[yq].astype(F32)

    agg_b = agg.T.astype(BF16)
    term = lax.dot_general(feat[...], agg_b, (((0,), (0,)), ((), ())), preferred_element_type=F32)
    for q in range(NG):
        for t in range(8):
            r0 = q * 32 + (t // 2) * 8
            w1[q, t] = term[r0:r0 + 8, (t % 2) * 128:(t % 2 + 1) * 128]

    def step(src_of, land, k, me, peer):
        for o in (1, 7, 2, 6, 3, 5, 4):
            q = (me + o) % 8
            start(src_of(q), land.at[me], g_ss.at[k, q], g_rs.at[k, me], peer(q))

    def take(land, k, me, peer):
        for o in (1, 7, 2, 6, 3, 5, 4):
            q = (me + o) % 8
            arrived(land.at[q], g_rs.at[k, q], peer(q))

    step(lambda q: w1.at[q], r1, 0, g, g_peer)
    gi[...] = lax.dot_general(
        agg_b, wgt[...], (((1,), (1,)), ((), ())), preferred_element_type=F32
    ).astype(BF16)
    r1[g] = w1[g]
    take(r1, 0, g, g_peer)
    s1[...] = jnp.sum(r1[...], axis=0)
    step(lambda q: s1.at[q], r2, 1, y, y_peer)
    r2[y] = s1[y]
    take(r2, 1, y, y_peer)
    s2[...] = jnp.sum(r2[...], axis=0)
    step(lambda q: s2, r3, 2, z, z_peer)
    r3[z] = s2[...]
    take(r3, 2, z, z_peer)
    f1[y] = jnp.sum(r3[...], axis=0)
    step(lambda q: f1.at[y], f1, 3, y, y_peer)
    take(f1, 3, y, y_peer)
    f2[g] = f1[...]
    step(lambda q: f1, f2, 4, g, g_peer)
    take(f2, 4, g, g_peer)
    for q in range(NG):
        for t in range(8):
            r0 = q * 32 + (t // 2) * 8
            gw[r0:r0 + 8, (t % 2) * 128:(t % 2 + 1) * 128] = f2[q, t]
    for copy in sent:
        copy.wait_send()


def body(grad_out, relu_mask, features, weight, tile_values, tile_lists, tile_count):
    lists = tile_lists[0, 0]
    place = (lists[1] - lax.axis_index("col") * BC) * BR + lists[0] - lax.axis_index("row") * BR
    live = jnp.arange(CAP, dtype=jnp.int32) < tile_count[0, 0]
    hit = (place[None, :] == jnp.arange(BR * BC, dtype=jnp.int32)[:, None]) & live[None, :]
    table = jnp.min(jnp.where(hit, lists[2][None, :], CAP), axis=1)
    vmem = pl.BlockSpec(memory_space=pltpu.VMEM)
    dma = pltpu.SemaphoreType.DMA
    gi, gw = pl.pallas_call(
        kernel,
        out_shape=(jax.ShapeDtypeStruct((BLOCK, D), BF16), jax.ShapeDtypeStruct((D, D), F32)),
        in_specs=[vmem, vmem, vmem, vmem, pl.BlockSpec(memory_space=pl.ANY),
                  pl.BlockSpec(memory_space=pltpu.SMEM)],
        out_specs=(vmem, vmem),
        scratch_shapes=[
            pltpu.VMEM((CAP + 1, BLOCK, BLOCK), BF16),
            pltpu.VMEM((BR, D, BLOCK), BF16),
            pltpu.VMEM((D, BR * BLOCK), BF16),
            pltpu.VMEM((BR * BLOCK, 2 * BLOCK), BF16),
            pltpu.VMEM((NZ, NYL, D, BLOCK), F32),
            pltpu.VMEM((2, 4, NYL, D, BLOCK), BF16),
            pltpu.VMEM((2, 4, NYL, D, BLOCK), BF16),
            pltpu.VMEM((D, BLOCK), F32),
            pltpu.VMEM((NYL, D, BLOCK), BF16),
            pltpu.VMEM((NYL, D, BLOCK), BF16),
            pltpu.VMEM((NG, 8, 8, 128), F32),
            pltpu.VMEM((NG, 8, 8, 128), F32),
            pltpu.VMEM((8, 8, 128), F32),
            pltpu.VMEM((NY, 8, 128), F32),
            pltpu.VMEM((8, 128), F32),
            pltpu.VMEM((NZ, 8, 128), F32),
            pltpu.VMEM((NY, 8, 128), F32),
            pltpu.VMEM((NG, 8, 8, 128), F32),
            dma((4,)),
            dma((15, PIECES)), dma((16, PIECES)),
            dma((2, 4, NYL)), dma((2, 4, NYL)),
            dma((NYL,)), dma((NYL,)),
            dma((5, 8)), dma((5, 8)),
        ],
        compiler_params=pltpu.CompilerParams(
            collective_id=0, has_side_effects=True, vmem_limit_bytes=48 * 1024 * 1024
        ),
    )(grad_out, relu_mask, features[0], weight, tile_values[0, 0], table)
    return gi[None], gw


def solution(mesh):
    return jax.shard_map(
        body,
        mesh=mesh,
        in_specs=(
            P(("row", "col"), None),
            P(("row", "col"), None),
            P("col", "row", None),
            P(),
            P("row", "col", None, None, None),
            P("row", "col", None, None),
            P("row", "col"),
        ),
        out_specs=(P("col", "row", None), P()),
        check_vma=False,
    )
```

```python
import jax
import jax.numpy as jnp
from jax import lax
from jax.experimental import pallas as pl
from jax.experimental.pallas import tpu as pltpu
from jax.sharding import PartitionSpec as P

NZ, NYL, NX, NY, NG = 8, 4, 4, 8, 8
BLOCK, D = 128, 256
BR, BC, CAP = 16, 32, 144
HALF = D // 2
EARLY, BEFORE = 6, 16
F32, BF16 = jnp.float32, jnp.bfloat16


def kernel(
    go_hbm, mask_hbm, feat_hbm, wgt_hbm, tiles, lists_hbm, count_hbm, gi, gw,
    go, mask, feat, wgt, lists, count, table_v, table, tiles_v,
    ag, dzall, part, zsend, zrecv, own, ysend, yrecv, feats, inner,
    w1, r1, s1, r2, s2, r3, f1, f1b, f2,
    in_sem, tile_sem, ag_ss, ag_rs, fy_ss, f_ss, f_rs, z_ss, z_rs,
    y_ss, y_rs, g_ss, g_rs,
):
    row, col = lax.axis_index("row"), lax.axis_index("col")
    ylo, z = row // NZ, row % NZ
    x, yh, core = col // 4, (col // 2) % 2, col % 2
    g = x * 2 + core
    y = yh * NYL + ylo

    def g_peer(q):
        return row, (q // 2) * 4 + yh * 2 + q % 2

    def y_peer(q):
        return (q % NYL) * NZ + z, x * 4 + (q // NYL) * 2 + core

    def z_peer(q):
        return ylo * NZ + q, col

    def yl_peer(q):
        return q * NZ + z, col

    def remote(src, dst, ssem, rsem, to):
        return pltpu.make_async_remote_copy(
            src_ref=src, dst_ref=dst, send_sem=ssem, recv_sem=rsem,
            device_id=to, device_id_type=pl.DeviceIdType.MESH,
        )

    sent = []

    def start(src, dst, ssem, rsem, to):
        copy = remote(src, dst, ssem, rsem, to)
        copy.start()
        sent.append(copy)

    def arrived(dst, sem, frm):
        remote(dst, dst, sem, sem, frm).wait_recv()

    barrier = pltpu.get_barrier_semaphore()
    for o in (4, 3, 5, 2, 6, 1, 7):
        for to in (y_peer((y + o) % NY), z_peer((z + o) % NZ), g_peer((g + o) % NG)):
            pl.semaphore_signal(barrier, inc=1, device_id=to, device_id_type=pl.DeviceIdType.MESH)
    fetched = []
    for i, (src, dst) in enumerate((
        (go_hbm, go), (mask_hbm, mask), (feat_hbm.at[0], feat), (wgt_hbm, wgt),
        (lists_hbm.at[0], lists), (count_hbm, count),
    )):
        copy = pltpu.make_async_copy(src, dst, in_sem.at[i])
        copy.start()
        fetched.append(copy)
    tile_copies = []
    for i in range(4):
        part_of = pl.ds(i * (CAP // 4), CAP // 4)
        copy = pltpu.make_async_copy(tiles.at[0, 0, part_of], tiles_v.at[part_of], tile_sem.at[i])
        copy.start()
        tile_copies.append(copy)
    fetched[0].wait()
    fetched[1].wait()
    dz = go[...].astype(F32) * mask[...].astype(F32)
    ag[col] = dz.T.astype(BF16)
    fetched[2].wait()
    feats[2, ylo] = feat[...].astype(F32).T.astype(BF16)
    pl.semaphore_wait(barrier, 21)

    def slot_of(xq, yq, cq):
        return xq * 4 + yq * 2 + cq

    def ag_send(slot, to_col, k):
        start(ag.at[slot], ag.at[slot], ag_ss.at[k], ag_rs.at[slot], (row, to_col))

    def ag_wait(slot, from_col):
        arrived(ag.at[slot], ag_rs.at[slot], (row, from_col))

    xs = [(x + o) % NX for o in (2, 1, 3)]
    over = slot_of(x, 1 - yh, core)
    ag_send(col, over, 0)
    for k, xq in enumerate(xs):
        ag_send(col, slot_of(xq, yh, core), 1 + k)
    ag_send(col, slot_of(x, yh, 1 - core), 4)
    fetched[4].wait()
    fetched[5].wait()
    tiles_v[CAP] = jnp.zeros((BLOCK, BLOCK), BF16)
    place = (lists[1] - col * BC) * BR + lists[0] - row * BR
    live = lax.broadcasted_iota(jnp.int32, (1, CAP), 1) < count[0, 0]
    place = jnp.broadcast_to(jnp.where(live, place, -1), (BLOCK, CAP)).T
    slots = jnp.broadcast_to(lists[2], (BLOCK, CAP)).T
    lane = lax.broadcasted_iota(jnp.int32, (CAP, BLOCK), 1)
    for b in range(NYL):
        table_v[b:b + 1] = jnp.min(
            jnp.where(place == lane + b * BLOCK, slots, CAP), axis=0, keepdims=True
        )
    table_copy = pltpu.make_async_copy(table_v, table, in_sem.at[6])
    table_copy.start()

    for o in (2, 1, 3):
        q = (ylo + o) % NYL
        start(feats.at[2, ylo], feats.at[2, ylo], fy_ss.at[q], f_rs.at[2, ylo], yl_peer(q))
    up, down = z_peer((z + 1) % NZ), z_peer((z + NZ - 1) % NZ)

    def feat_along(yq, src_up, src_down):
        for src, dst, to in ((src_up, src_up - 1, up), (src_down, src_down + 1, down)):
            start(feats.at[src, yq], feats.at[dst, yq], f_ss.at[dst, yq], f_rs.at[dst, yq], to)

    def feat_wait(at, yq, frm):
        arrived(feats.at[at, yq], f_rs.at[at, yq], frm)

    ag_wait(over, over)
    for k, xq in enumerate(xs):
        ag_send(over, slot_of(xq, yh, core), 5 + k)
    ag_send(over, slot_of(x, yh, 1 - core), 8)
    for k, xq in enumerate(xs):
        ag_wait(slot_of(xq, yh, core), slot_of(xq, yh, core))
        ag_send(slot_of(xq, yh, core), slot_of(x, yh, 1 - core), 9 + k)

    sides = (yh, 1 - yh)

    def fill(side):
        for k in range(8):
            at = (side * 8 + k) * BLOCK
            dzall[:, at:at + BLOCK] = ag[slot_of(k // 2, sides[side], k % 2)]

    def product(zq, h, side):
        first = zq * BR + sides[side] * 2
        rhs = jnp.concatenate([
            jnp.concatenate(
                [tiles_v[table[2 * h + j, first + (k // 2) * 4 + k % 2]] for k in range(8)], axis=0
            )
            for j in range(2)
        ], axis=1)
        lhs = dzall[:, side * 8 * BLOCK:(side + 1) * 8 * BLOCK]
        return jnp.dot(lhs, rhs, preferred_element_type=F32)

    def first_half(t, carry):
        zq, h = t // 2, t % 2
        res = product(zq, h, 0)
        part[zq, 2 * h] = res[:, :BLOCK]
        part[zq, 2 * h + 1] = res[:, BLOCK:]
        return carry

    for xq in range(NX):
        ag_wait(slot_of(xq, yh, 1 - core), slot_of(x, yh, 1 - core))
    table_copy.wait()
    for copy in tile_copies + fetched[3:4]:
        copy.wait()
    fill(0)
    lax.fori_loop(0, EARLY, first_half, 0)
    for o in (0, 1, 3, 2):
        q = (ylo + o) % NYL
        if o:
            feat_wait(2, q, yl_peer(q))
        feat_along(q, 2, 2)
    lax.fori_loop(EARLY, BEFORE, first_half, 0)
    for k, xq in enumerate(xs):
        ag_wait(slot_of(xq, 1 - yh, core), slot_of(xq, yh, core))
        ag_send(slot_of(xq, 1 - yh, core), slot_of(x, yh, 1 - core), 12 + k)
    if BEFORE < 2 * NZ:
        lax.fori_loop(BEFORE, 2 * NZ, first_half, 0)
    for xq in range(NX):
        ag_wait(slot_of(xq, 1 - yh, 1 - core), slot_of(x, yh, 1 - core))
    fill(1)

    def compute(zq):
        def second_half(h, carry):
            res = product(zq, h, 1)
            part[zq, 2 * h] += res[:, :BLOCK]
            part[zq, 2 * h + 1] += res[:, BLOCK:]
            return carry

        lax.fori_loop(0, NYL // 2, second_half, 0)
    ways = (up, down)
    order = [(ylo + o) % NYL for o in (2, 1, 3, 0)]

    def chain(s):
        for yq in order:
            for d in range(2):
                dest = (z + 4 - s) % NZ if d == 0 else (z + 4 + s) % NZ
                mine = pl.ds(d * HALF, HALF)
                if s == 0:
                    zsend[d, s, yq, mine] = part[dest, yq, mine].astype(BF16)
                    src, dst = zsend.at[d, s, yq, mine], zrecv.at[d, s, yq, mine]
                elif s == 1:
                    arrived(zrecv.at[d, 0, yq, mine], z_rs.at[d, 0, yq], ways[1 - d])
                    other = pl.ds((1 - d) * HALF, HALF)
                    got = part[dest, yq, mine] + zrecv[d, 0, yq, mine].astype(F32)
                    zsend[d, s, yq, mine] = got.astype(BF16)
                    zsend[d, s, yq, other] = part[dest, yq, other].astype(BF16)
                    src, dst = zsend.at[d, s, yq], zrecv.at[d, s, yq]
                else:
                    arrived(zrecv.at[d, s - 1, yq], z_rs.at[d, s - 1, yq], ways[1 - d])
                    got = part[dest, yq] + zrecv[d, s - 1, yq].astype(F32)
                    zsend[d, s, yq] = got.astype(BF16)
                    src, dst = zsend.at[d, s, yq], zrecv.at[d, s, yq]
                start(src, dst, z_ss.at[d, s, yq], z_rs.at[d, s, yq], ways[d])

    def weight_term(lefts, rights):
        return lax.dot_general(
            jnp.concatenate(lefts, axis=1), jnp.concatenate(rights, axis=1),
            (((1,), (1,)), ((), ())), preferred_element_type=F32,
        )

    compute((z + 4) % NZ)
    chain(0)
    for yq in order[::-1]:
        feat_wait(1, yq, down)
        feat_wait(3, yq, up)
        feat_along(yq, 1, 3)
    compute((z + 3) % NZ)
    compute((z + 5) % NZ)
    chain(1)
    for o in (2, 6, 1, 7, 0):
        compute((z + o) % NZ)
    inner[...] = weight_term(
        [feats[2 + i, q] for i in (-1, 0, 1) for q in range(NYL)],
        [part[(z + NZ + i) % NZ, q].astype(BF16) for i in (-1, 0, 1) for q in range(NYL)],
    )
    chain(2)
    for yq in order[::-1]:
        feat_wait(0, yq, down)
        feat_wait(4, yq, up)
    term = (inner[...] + weight_term(
        [feats[i, q] for i in (4, 0) for q in range(NYL)],
        [zsend[d, 2, q] for d in range(2) for q in range(NYL)],
    )).astype(BF16)
    for q in range(NG):
        w1[q, :32] = term[q * 32:(q + 1) * 32, :128]
        w1[q, 32:] = term[q * 32:(q + 1) * 32, 128:]

    def step(src_of, land, k, me, peer):
        for o in (4, 3, 5, 2, 6, 1, 7):
            q = (me + o) % 8
            start(src_of(q), land.at[me], g_ss.at[k, q], g_rs.at[k, me], peer(q))

    def take(land, k, me, peer):
        for o in (1, 7, 2, 6, 3, 5, 4):
            q = (me + o) % 8
            arrived(land.at[q], g_rs.at[k, q], peer(q))

    step(lambda q: w1.at[q], r1, 0, g, g_peer)
    r1[g] = w1[g]
    take(r1, 0, g, g_peer)
    s1[...] = jnp.sum(r1[...].astype(F32), axis=0)
    step(lambda q: s1.at[pl.ds(pl.multiple_of(q * 8, 8), 8)], r2, 1, y, y_peer)
    r2[y] = s1[pl.ds(pl.multiple_of(y * 8, 8), 8)]
    chain(3)
    take(r2, 1, y, y_peer)
    s2[...] = jnp.sum(r2[...], axis=0)
    step(lambda q: s2, r3, 2, z, z_peer)
    r3[z] = s2[...]
    take(r3, 2, z, z_peer)
    f1[y] = jnp.sum(r3[...], axis=0)
    step(lambda q: f1.at[y], f1, 3, y, y_peer)
    for k, yq in enumerate(order):
        for d in range(2):
            arrived(zrecv.at[d, 3, yq], z_rs.at[d, 3, yq], ways[1 - d])
        total = part[z, yq] + zrecv[0, 3, yq].astype(F32) + zrecv[1, 3, yq].astype(F32)
        if k < 3:
            ysend[yq] = total.astype(BF16)
            start(ysend.at[yq], yrecv.at[ylo], y_ss.at[yq], y_rs.at[ylo], yl_peer(yq))
        else:
            own[...] = total
    take(f1, 3, y, y_peer)
    f1b[...] = f1[...].reshape(64, 128).astype(BF16)
    f2[g] = f1b[...]
    step(lambda q: f1b, f2, 4, g, g_peer)

    agg = own[...]
    for yq in order[:3]:
        arrived(yrecv.at[yq], y_rs.at[yq], yl_peer(yq))
        agg = agg + yrecv[yq].astype(F32)
    gi[...] = lax.dot_general(
        agg.T.astype(BF16), wgt[...], (((1,), (1,)), ((), ())), preferred_element_type=F32
    ).astype(BF16)
    take(f2, 4, g, g_peer)
    for q in range(NG):
        gw[q * 32:(q + 1) * 32, :128] = f2[q, :32].astype(F32)
        gw[q * 32:(q + 1) * 32, 128:] = f2[q, 32:].astype(F32)
    for copy in sent:
        copy.wait_send()


def body(grad_out, relu_mask, features, weight, tile_values, tile_lists, tile_count):
    vmem = pl.BlockSpec(memory_space=pltpu.VMEM)
    dma = pltpu.SemaphoreType.DMA
    gi, gw = pl.pallas_call(
        kernel,
        out_shape=(jax.ShapeDtypeStruct((BLOCK, D), BF16), jax.ShapeDtypeStruct((D, D), F32)),
        in_specs=[pl.BlockSpec(memory_space=pl.ANY)] * 7,
        out_specs=(vmem, vmem),
        scratch_shapes=[
            pltpu.VMEM((BLOCK, D), BF16),
            pltpu.VMEM((BLOCK, D), jnp.int32),
            pltpu.VMEM((BLOCK, D), BF16),
            pltpu.VMEM((D, D), BF16),
            pltpu.VMEM((3, 1, CAP), jnp.int32),
            pltpu.SMEM((1, 1), jnp.int32),
            pltpu.VMEM((NYL, BLOCK), jnp.int32),
            pltpu.SMEM((NYL, BLOCK), jnp.int32),
            pltpu.VMEM((CAP + 1, BLOCK, BLOCK), BF16),
            pltpu.VMEM((BR, D, BLOCK), BF16),
            pltpu.VMEM((D, BR * BLOCK), BF16),
            pltpu.VMEM((NZ, NYL, D, BLOCK), F32),
            pltpu.VMEM((2, 4, NYL, D, BLOCK), BF16),
            pltpu.VMEM((2, 4, NYL, D, BLOCK), BF16),
            pltpu.VMEM((D, BLOCK), F32),
            pltpu.VMEM((NYL, D, BLOCK), BF16),
            pltpu.VMEM((NYL, D, BLOCK), BF16),
            pltpu.VMEM((5, NYL, D, BLOCK), BF16),
            pltpu.VMEM((D, D), F32),
            pltpu.VMEM((NG, 64, 128), BF16),
            pltpu.VMEM((NG, 64, 128), BF16),
            pltpu.VMEM((64, 128), F32),
            pltpu.VMEM((NY, 8, 128), F32),
            pltpu.VMEM((8, 128), F32),
            pltpu.VMEM((NZ, 8, 128), F32),
            pltpu.VMEM((NY, 8, 128), F32),
            pltpu.VMEM((64, 128), BF16),
            pltpu.VMEM((NG, 64, 128), BF16),
            dma((7,)), dma((4,)),
            dma((15,)), dma((16,)),
            dma((NYL,)), dma((5, NYL)), dma((5, NYL)),
            dma((2, 4, NYL)), dma((2, 4, NYL)),
            dma((NYL,)), dma((NYL,)),
            dma((5, 8)), dma((5, 8)),
        ],
        compiler_params=pltpu.CompilerParams(
            collective_id=0, has_side_effects=True, vmem_limit_bytes=48 * 1024 * 1024
        ),
    )(
        *(pltpu.with_memory_space_constraint(a, pltpu.HBM) for a in (
            grad_out, relu_mask, features, weight, tile_values, tile_lists.transpose(0, 2, 1, 3)
        )),
        tile_count,
    )
    return gi[None], gw


def solution(mesh):
    return jax.shard_map(
        body,
        mesh=mesh,
        in_specs=(
            P(("row", "col"), None),
            P(("row", "col"), None),
            P("col", "row", None),
            P(),
            P("row", "col", None, None, None),
            P("row", "col", None, None),
            P("row", "col"),
        ),
        out_specs=(P("col", "row", None), P()),
        check_vma=False,
    )
```

```python
import jax
import jax.numpy as jnp
from jax import lax
from jax.experimental import pallas as pl
from jax.experimental.pallas import tpu as pltpu
from jax.sharding import PartitionSpec as P

NZ, NYL, NX, NY, NG = 8, 4, 4, 8, 8
BLOCK, D = 128, 256
BR, BC, CAP = 16, 32, 144
HALF = D // 2
EARLY, BEFORE = 2, 8
F32, BF16 = jnp.float32, jnp.bfloat16


def kernel(
    go_hbm, mask_hbm, feat_hbm, wgt_hbm, tiles, lists_hbm, count_hbm, gi, gw,
    go, mask, feat, wgt, lists, count, table_v, table, tiles_v,
    ag, dzall, part, zsend, zrecv, own, ysend, yrecv, feats, inner,
    w1, r1, s1, r2, s2, r3, f1, f1b, f2,
    in_sem, tile_sem, ag_ss, ag_rs, fy_ss, f_ss, f_rs, z_ss, z_rs,
    y_ss, y_rs, g_ss, g_rs,
):
    row, col = lax.axis_index("row"), lax.axis_index("col")
    ylo, z = row // NZ, row % NZ
    x, yh, core = col // 4, (col // 2) % 2, col % 2
    g = x * 2 + core
    y = yh * NYL + ylo

    def g_peer(q):
        return row, (q // 2) * 4 + yh * 2 + q % 2

    def y_peer(q):
        return (q % NYL) * NZ + z, x * 4 + (q // NYL) * 2 + core

    def z_peer(q):
        return ylo * NZ + q, col

    def yl_peer(q):
        return q * NZ + z, col

    def remote(src, dst, ssem, rsem, to):
        return pltpu.make_async_remote_copy(
            src_ref=src, dst_ref=dst, send_sem=ssem, recv_sem=rsem,
            device_id=to, device_id_type=pl.DeviceIdType.MESH,
        )

    sent = []

    def start(src, dst, ssem, rsem, to):
        copy = remote(src, dst, ssem, rsem, to)
        copy.start()
        sent.append(copy)

    def arrived(dst, sem, frm):
        remote(dst, dst, sem, sem, frm).wait_recv()

    barrier = pltpu.get_barrier_semaphore()
    for o in (4, 3, 5, 2, 6, 1, 7):
        for to in (y_peer((y + o) % NY), z_peer((z + o) % NZ), g_peer((g + o) % NG)):
            pl.semaphore_signal(barrier, inc=1, device_id=to, device_id_type=pl.DeviceIdType.MESH)
    fetched = []
    for i, (src, dst) in enumerate((
        (go_hbm, go), (mask_hbm, mask), (feat_hbm.at[0], feat), (wgt_hbm, wgt),
        (lists_hbm.at[0], lists), (count_hbm, count),
    )):
        copy = pltpu.make_async_copy(src, dst, in_sem.at[i])
        copy.start()
        fetched.append(copy)
    tile_copies = []
    for i in range(4):
        part_of = pl.ds(i * (CAP // 4), CAP // 4)
        copy = pltpu.make_async_copy(tiles.at[0, 0, part_of], tiles_v.at[part_of], tile_sem.at[i])
        copy.start()
        tile_copies.append(copy)
    fetched[0].wait()
    fetched[1].wait()
    dz = go[...].astype(F32) * mask[...].astype(F32)
    ag[col] = dz.T.astype(BF16)
    fetched[2].wait()
    feats[2, ylo] = feat[...].astype(F32).T.astype(BF16)
    fetched[4].wait()
    fetched[5].wait()
    tiles_v[CAP] = jnp.zeros((BLOCK, BLOCK), BF16)
    place = (lists[1] - col * BC) * BR + lists[0] - row * BR
    live = lax.broadcasted_iota(jnp.int32, (1, CAP), 1) < count[0, 0]
    place = jnp.broadcast_to(jnp.where(live, place, -1), (BLOCK, CAP)).T
    slots = jnp.broadcast_to(lists[2], (BLOCK, CAP)).T
    lane = lax.broadcasted_iota(jnp.int32, (CAP, BLOCK), 1)
    for b in range(NYL):
        table_v[b:b + 1] = jnp.min(
            jnp.where(place == lane + b * BLOCK, slots, CAP), axis=0, keepdims=True
        )
    table_copy = pltpu.make_async_copy(table_v, table, in_sem.at[6])
    table_copy.start()
    pl.semaphore_wait(barrier, 21)

    def slot_of(xq, yq, cq):
        return xq * 4 + yq * 2 + cq

    def ag_send(slot, to_col, k):
        start(ag.at[slot], ag.at[slot], ag_ss.at[k], ag_rs.at[slot], (row, to_col))

    def ag_wait(slot, from_col):
        arrived(ag.at[slot], ag_rs.at[slot], (row, from_col))

    xs = [(x + o) % NX for o in (2, 1, 3)]
    over = slot_of(x, 1 - yh, core)
    ag_send(col, over, 0)
    for k, xq in enumerate(xs):
        ag_send(col, slot_of(xq, yh, core), 1 + k)
    ag_send(col, slot_of(x, yh, 1 - core), 4)
    up, down = z_peer((z + 1) % NZ), z_peer((z + NZ - 1) % NZ)
    up2, down2 = z_peer((z + 2) % NZ), z_peer((z + NZ - 2) % NZ)
    for dst, to in ((0, up2), (4, down2)):
        start(feats.at[2, ylo], feats.at[dst, ylo], f_ss.at[dst, ylo], f_rs.at[dst, ylo], to)

    def feat_over_y(at):
        for o in (2, 1, 3):
            q = (ylo + o) % NYL
            start(feats.at[at, ylo], feats.at[at, ylo], fy_ss.at[at, q], f_rs.at[at, ylo], yl_peer(q))

    feat_over_y(2)

    def feat_along(yq):
        for dst, to in ((1, up), (3, down)):
            start(feats.at[2, yq], feats.at[dst, yq], f_ss.at[dst, yq], f_rs.at[dst, yq], to)

    def feat_wait(at, yq, frm):
        arrived(feats.at[at, yq], f_rs.at[at, yq], frm)

    ag_wait(over, over)
    for k, xq in enumerate(xs):
        ag_send(over, slot_of(xq, yh, core), 5 + k)
    ag_send(over, slot_of(x, yh, 1 - core), 8)
    for k, xq in enumerate(xs):
        ag_wait(slot_of(xq, yh, core), slot_of(xq, yh, core))
        ag_send(slot_of(xq, yh, core), slot_of(x, yh, 1 - core), 9 + k)

    feat_along(ylo)

    sides = (yh, 1 - yh)

    def fill(side):
        for k in range(8):
            at = (side * 8 + k) * BLOCK
            dzall[:, at:at + BLOCK] = ag[slot_of(k // 2, sides[side], k % 2)]

    def product(zq, h, side):
        first = zq * BR + sides[side] * 2
        rhs = jnp.concatenate([
            jnp.concatenate(
                [tiles_v[table[2 * h + j, first + (k // 2) * 4 + k % 2]] for k in range(8)], axis=0
            )
            for j in range(2)
        ], axis=1)
        lhs = dzall[:, side * 8 * BLOCK:(side + 1) * 8 * BLOCK]
        return jnp.dot(lhs, rhs, preferred_element_type=F32)

    def first_half(t, carry):
        zq, h = t // 2, t % 2
        res = product(zq, h, 0)
        part[zq, 2 * h] = res[:, :BLOCK]
        part[zq, 2 * h + 1] = res[:, BLOCK:]
        return carry

    for xq in range(NX):
        ag_wait(slot_of(xq, yh, 1 - core), slot_of(x, yh, 1 - core))
    table_copy.wait()
    for copy in tile_copies + fetched[3:4]:
        copy.wait()
    fill(0)
    lax.fori_loop(0, EARLY, first_half, 0)
    lax.fori_loop(EARLY, BEFORE, first_half, 0)
    for k, xq in enumerate(xs):
        ag_wait(slot_of(xq, 1 - yh, core), slot_of(xq, yh, core))
        ag_send(slot_of(xq, 1 - yh, core), slot_of(x, yh, 1 - core), 12 + k)
    for o in (1, 3, 2):
        q = (ylo + o) % NYL
        feat_wait(2, q, yl_peer(q))
        feat_along(q)
    feat_wait(0, ylo, down2)
    feat_wait(4, ylo, up2)
    feat_over_y(0)
    feat_over_y(4)
    if BEFORE < 2 * NZ:
        lax.fori_loop(BEFORE, 2 * NZ, first_half, 0)
    for xq in range(NX):
        ag_wait(slot_of(xq, 1 - yh, 1 - core), slot_of(x, yh, 1 - core))
    fill(1)

    def compute(zq):
        def second_half(h, carry):
            res = product(zq, h, 1)
            part[zq, 2 * h] += res[:, :BLOCK]
            part[zq, 2 * h + 1] += res[:, BLOCK:]
            return carry

        lax.fori_loop(0, NYL // 2, second_half, 0)
    ways = (up, down)
    order = [(ylo + o) % NYL for o in (2, 1, 3, 0)]

    def chain(s):
        for yq in order:
            for d in range(2):
                dest = (z + 4 - s) % NZ if d == 0 else (z + 4 + s) % NZ
                mine = pl.ds(d * HALF, HALF)
                if s == 0:
                    zsend[d, s, yq, mine] = part[dest, yq, mine].astype(BF16)
                    src, dst = zsend.at[d, s, yq, mine], zrecv.at[d, s, yq, mine]
                elif s == 1:
                    arrived(zrecv.at[d, 0, yq, mine], z_rs.at[d, 0, yq], ways[1 - d])
                    other = pl.ds((1 - d) * HALF, HALF)
                    got = part[dest, yq, mine] + zrecv[d, 0, yq, mine].astype(F32)
                    zsend[d, s, yq, mine] = got.astype(BF16)
                    zsend[d, s, yq, other] = part[dest, yq, other].astype(BF16)
                    src, dst = zsend.at[d, s, yq], zrecv.at[d, s, yq]
                else:
                    arrived(zrecv.at[d, s - 1, yq], z_rs.at[d, s - 1, yq], ways[1 - d])
                    got = part[dest, yq] + zrecv[d, s - 1, yq].astype(F32)
                    zsend[d, s, yq] = got.astype(BF16)
                    src, dst = zsend.at[d, s, yq], zrecv.at[d, s, yq]
                start(src, dst, z_ss.at[d, s, yq], z_rs.at[d, s, yq], ways[d])

    def weight_term(lefts, rights):
        return lax.dot_general(
            jnp.concatenate(lefts, axis=1), jnp.concatenate(rights, axis=1),
            (((1,), (1,)), ((), ())), preferred_element_type=F32,
        )

    compute((z + 4) % NZ)
    chain(0)
    compute((z + 3) % NZ)
    compute((z + 5) % NZ)
    chain(1)
    for o in (2, 6, 1, 7, 0):
        compute((z + o) % NZ)
    for yq in order[::-1]:
        feat_wait(1, yq, down)
        feat_wait(3, yq, up)
    inner[...] = weight_term(
        [feats[2 + i, q] for i in (-1, 0, 1) for q in range(NYL)],
        [part[(z + NZ + i) % NZ, q].astype(BF16) for i in (-1, 0, 1) for q in range(NYL)],
    )
    chain(2)
    for yq in order[:3]:
        feat_wait(0, yq, yl_peer(yq))
        feat_wait(4, yq, yl_peer(yq))
    term = (inner[...] + weight_term(
        [feats[i, q] for i in (4, 0) for q in range(NYL)],
        [zsend[d, 2, q] for d in range(2) for q in range(NYL)],
    )).astype(BF16)
    for q in range(NG):
        w1[q, :32] = term[q * 32:(q + 1) * 32, :128]
        w1[q, 32:] = term[q * 32:(q + 1) * 32, 128:]

    def step(src_of, land, k, me, peer):
        for o in (4, 3, 5, 2, 6, 1, 7):
            q = (me + o) % 8
            start(src_of(q), land.at[me], g_ss.at[k, q], g_rs.at[k, me], peer(q))

    def take(land, k, me, peer):
        for o in (1, 7, 2, 6, 3, 5, 4):
            q = (me + o) % 8
            arrived(land.at[q], g_rs.at[k, q], peer(q))

    step(lambda q: w1.at[q], r1, 0, g, g_peer)
    r1[g] = w1[g]
    take(r1, 0, g, g_peer)
    s1[...] = jnp.sum(r1[...].astype(F32), axis=0)
    step(lambda q: s1.at[pl.ds(pl.multiple_of(q * 8, 8), 8)], r2, 1, y, y_peer)
    r2[y] = s1[pl.ds(pl.multiple_of(y * 8, 8), 8)]
    chain(3)
    take(r2, 1, y, y_peer)
    s2[...] = jnp.sum(r2[...], axis=0)
    step(lambda q: s2, r3, 2, z, z_peer)
    r3[z] = s2[...]
    take(r3, 2, z, z_peer)
    f1[y] = jnp.sum(r3[...], axis=0)
    step(lambda q: f1.at[y], f1, 3, y, y_peer)
    for k, yq in enumerate(order):
        for d in range(2):
            arrived(zrecv.at[d, 3, yq], z_rs.at[d, 3, yq], ways[1 - d])
        total = part[z, yq] + zrecv[0, 3, yq].astype(F32) + zrecv[1, 3, yq].astype(F32)
        if k < 3:
            ysend[yq] = total.astype(BF16)
            start(ysend.at[yq], yrecv.at[ylo], y_ss.at[yq], y_rs.at[ylo], yl_peer(yq))
        else:
            own[...] = total
    take(f1, 3, y, y_peer)
    f1b[...] = f1[...].reshape(64, 128).astype(BF16)
    f2[g] = f1b[...]
    step(lambda q: f1b, f2, 4, g, g_peer)

    agg = own[...]
    for yq in order[:3]:
        arrived(yrecv.at[yq], y_rs.at[yq], yl_peer(yq))
        agg = agg + yrecv[yq].astype(F32)
    gi[...] = lax.dot_general(
        agg.T.astype(BF16), wgt[...], (((1,), (1,)), ((), ())), preferred_element_type=F32
    ).astype(BF16)
    take(f2, 4, g, g_peer)
    for q in range(NG):
        gw[q * 32:(q + 1) * 32, :128] = f2[q, :32].astype(F32)
        gw[q * 32:(q + 1) * 32, 128:] = f2[q, 32:].astype(F32)
    for copy in sent:
        copy.wait_send()


def body(grad_out, relu_mask, features, weight, tile_values, tile_lists, tile_count):
    vmem = pl.BlockSpec(memory_space=pltpu.VMEM)
    dma = pltpu.SemaphoreType.DMA
    gi, gw = pl.pallas_call(
        kernel,
        out_shape=(jax.ShapeDtypeStruct((BLOCK, D), BF16), jax.ShapeDtypeStruct((D, D), F32)),
        in_specs=[pl.BlockSpec(memory_space=pl.ANY)] * 7,
        out_specs=(vmem, vmem),
        scratch_shapes=[
            pltpu.VMEM((BLOCK, D), BF16),
            pltpu.VMEM((BLOCK, D), jnp.int32),
            pltpu.VMEM((BLOCK, D), BF16),
            pltpu.VMEM((D, D), BF16),
            pltpu.VMEM((3, 1, CAP), jnp.int32),
            pltpu.SMEM((1, 1), jnp.int32),
            pltpu.VMEM((NYL, BLOCK), jnp.int32),
            pltpu.SMEM((NYL, BLOCK), jnp.int32),
            pltpu.VMEM((CAP + 1, BLOCK, BLOCK), BF16),
            pltpu.VMEM((BR, D, BLOCK), BF16),
            pltpu.VMEM((D, BR * BLOCK), BF16),
            pltpu.VMEM((NZ, NYL, D, BLOCK), F32),
            pltpu.VMEM((2, 4, NYL, D, BLOCK), BF16),
            pltpu.VMEM((2, 4, NYL, D, BLOCK), BF16),
            pltpu.VMEM((D, BLOCK), F32),
            pltpu.VMEM((NYL, D, BLOCK), BF16),
            pltpu.VMEM((NYL, D, BLOCK), BF16),
            pltpu.VMEM((5, NYL, D, BLOCK), BF16),
            pltpu.VMEM((D, D), F32),
            pltpu.VMEM((NG, 64, 128), BF16),
            pltpu.VMEM((NG, 64, 128), BF16),
            pltpu.VMEM((64, 128), F32),
            pltpu.VMEM((NY, 8, 128), F32),
            pltpu.VMEM((8, 128), F32),
            pltpu.VMEM((NZ, 8, 128), F32),
            pltpu.VMEM((NY, 8, 128), F32),
            pltpu.VMEM((64, 128), BF16),
            pltpu.VMEM((NG, 64, 128), BF16),
            dma((7,)), dma((4,)),
            dma((15,)), dma((16,)),
            dma((5, NYL)), dma((5, NYL)), dma((5, NYL)),
            dma((2, 4, NYL)), dma((2, 4, NYL)),
            dma((NYL,)), dma((NYL,)),
            dma((5, 8)), dma((5, 8)),
        ],
        compiler_params=pltpu.CompilerParams(
            collective_id=0, has_side_effects=True, vmem_limit_bytes=48 * 1024 * 1024
        ),
    )(
        *(pltpu.with_memory_space_constraint(a, pltpu.HBM) for a in (
            grad_out, relu_mask, features, weight, tile_values, tile_lists.transpose(0, 2, 1, 3)
        )),
        tile_count,
    )
    return gi[None], gw


def solution(mesh):
    return jax.shard_map(
        body,
        mesh=mesh,
        in_specs=(
            P(("row", "col"), None),
            P(("row", "col"), None),
            P("col", "row", None),
            P(),
            P("row", "col", None, None, None),
            P("row", "col", None, None),
            P("row", "col"),
        ),
        out_specs=(P("col", "row", None), P()),
        check_vma=False,
    )
```

```python
import jax
import jax.numpy as jnp
from jax import lax
from jax.experimental import pallas as pl
from jax.experimental.pallas import tpu as pltpu
from jax.sharding import PartitionSpec as P

NZ, NYL, NX, NY, NG = 8, 4, 4, 8, 8
BLOCK, D = 128, 256
BR, BC, CAP = 16, 32, 144
HALF = D // 2
EARLY, BEFORE = 2, 8
F32, BF16 = jnp.float32, jnp.bfloat16


def kernel(
    go_hbm, mask_hbm, feat_hbm, wgt_hbm, tiles, lists_hbm, count_hbm, gi, gw,
    go, mask, feat, wgt, lists, count, table_v, table, tiles_v,
    ag, dzall, part, zsend, zrecv, own, ysend, yrecv, feats, inner,
    w1, r1, s1, r2, s2, r3, f1, f1b, f2,
    in_sem, tile_sem, ag_ss, ag_rs, fy_ss, f_ss, f_rs, z_ss, z_rs,
    y_ss, y_rs, g_ss, g_rs,
):
    row, col = lax.axis_index("row"), lax.axis_index("col")
    ylo, z = row // NZ, row % NZ
    x, yh, core = col // 4, (col // 2) % 2, col % 2
    g = x * 2 + core
    y = yh * NYL + ylo

    def g_peer(q):
        return row, (q // 2) * 4 + yh * 2 + q % 2

    def y_peer(q):
        return (q % NYL) * NZ + z, x * 4 + (q // NYL) * 2 + core

    def z_peer(q):
        return ylo * NZ + q, col

    def yl_peer(q):
        return q * NZ + z, col

    def remote(src, dst, ssem, rsem, to):
        return pltpu.make_async_remote_copy(
            src_ref=src, dst_ref=dst, send_sem=ssem, recv_sem=rsem,
            device_id=to, device_id_type=pl.DeviceIdType.MESH,
        )

    sent = []

    def start(src, dst, ssem, rsem, to):
        copy = remote(src, dst, ssem, rsem, to)
        copy.start()
        sent.append(copy)

    def arrived(dst, sem, frm):
        remote(dst, dst, sem, sem, frm).wait_recv()

    barrier = pltpu.get_barrier_semaphore()
    for o in (4, 3, 5, 2, 6, 1, 7):
        for to in (y_peer((y + o) % NY), z_peer((z + o) % NZ), g_peer((g + o) % NG)):
            pl.semaphore_signal(barrier, inc=1, device_id=to, device_id_type=pl.DeviceIdType.MESH)
    fetched = []
    for i, (src, dst) in enumerate((
        (go_hbm, go), (mask_hbm, mask), (feat_hbm.at[0], feat), (wgt_hbm, wgt),
        (lists_hbm.at[0], lists), (count_hbm, count),
    )):
        copy = pltpu.make_async_copy(src, dst, in_sem.at[i])
        copy.start()
        fetched.append(copy)
    tile_copies = []
    for i in range(4):
        part_of = pl.ds(i * (CAP // 4), CAP // 4)
        copy = pltpu.make_async_copy(tiles.at[0, 0, part_of], tiles_v.at[part_of], tile_sem.at[i])
        copy.start()
        tile_copies.append(copy)
    fetched[0].wait()
    fetched[1].wait()
    dz = go[...].astype(F32) * mask[...].astype(F32)
    ag[col] = dz.T.astype(BF16)
    fetched[2].wait()
    feats[2, ylo] = feat[...].astype(F32).T.astype(BF16)
    fetched[4].wait()
    fetched[5].wait()
    tiles_v[CAP] = jnp.zeros((BLOCK, BLOCK), BF16)
    place = (lists[1] - col * BC) * BR + lists[0] - row * BR
    live = lax.broadcasted_iota(jnp.int32, (1, CAP), 1) < count[0, 0]
    place = jnp.broadcast_to(jnp.where(live, place, -1), (BLOCK, CAP)).T
    slots = jnp.broadcast_to(lists[2], (BLOCK, CAP)).T
    lane = lax.broadcasted_iota(jnp.int32, (CAP, BLOCK), 1)
    for b in range(NYL):
        table_v[b:b + 1] = jnp.min(
            jnp.where(place == lane + b * BLOCK, slots, CAP), axis=0, keepdims=True
        )
    table_copy = pltpu.make_async_copy(table_v, table, in_sem.at[6])
    table_copy.start()
    pl.semaphore_wait(barrier, 21)

    def slot_of(xq, yq, cq):
        return xq * 4 + yq * 2 + cq

    def ag_send(slot, to_col, k):
        start(ag.at[slot], ag.at[slot], ag_ss.at[k], ag_rs.at[slot], (row, to_col))

    def ag_wait(slot, from_col):
        arrived(ag.at[slot], ag_rs.at[slot], (row, from_col))

    xs = [(x + o) % NX for o in (2, 1, 3)]
    over = slot_of(x, 1 - yh, core)
    ag_send(col, over, 0)
    for k, xq in enumerate(xs):
        ag_send(col, slot_of(xq, yh, core), 1 + k)
    ag_send(col, slot_of(x, yh, 1 - core), 4)
    up, down = z_peer((z + 1) % NZ), z_peer((z + NZ - 1) % NZ)
    up2, down2 = z_peer((z + 2) % NZ), z_peer((z + NZ - 2) % NZ)
    for dst, to in ((0, up2), (4, down2)):
        start(feats.at[2, ylo], feats.at[dst, ylo], f_ss.at[dst, ylo], f_rs.at[dst, ylo], to)

    def feat_over_y(at):
        for o in (2, 1, 3):
            q = (ylo + o) % NYL
            start(feats.at[at, ylo], feats.at[at, ylo], fy_ss.at[at, q], f_rs.at[at, ylo], yl_peer(q))

    feat_over_y(2)

    def feat_along(yq):
        for dst, to in ((1, up), (3, down)):
            start(feats.at[2, yq], feats.at[dst, yq], f_ss.at[dst, yq], f_rs.at[dst, yq], to)

    def feat_wait(at, yq, frm):
        arrived(feats.at[at, yq], f_rs.at[at, yq], frm)

    ag_wait(over, over)
    for k, xq in enumerate(xs):
        ag_send(over, slot_of(xq, yh, core), 5 + k)
    ag_send(over, slot_of(x, yh, 1 - core), 8)
    for k, xq in enumerate(xs):
        ag_wait(slot_of(xq, yh, core), slot_of(xq, yh, core))
        ag_send(slot_of(xq, yh, core), slot_of(x, yh, 1 - core), 9 + k)

    feat_along(ylo)

    sides = (yh, 1 - yh)

    def fill(side):
        for k in range(8):
            at = (side * 8 + k) * BLOCK
            dzall[:, at:at + BLOCK] = ag[slot_of(k // 2, sides[side], k % 2)]

    def product(zq, h, side):
        first = zq * BR + sides[side] * 2
        rhs = jnp.concatenate([
            jnp.concatenate(
                [tiles_v[table[2 * h + j, first + (k // 2) * 4 + k % 2]] for k in range(8)], axis=0
            )
            for j in range(2)
        ], axis=1)
        lhs = dzall[:, side * 8 * BLOCK:(side + 1) * 8 * BLOCK]
        return jnp.dot(lhs, rhs, preferred_element_type=F32)

    def first_half(t, carry):
        zq, h = t // 2, t % 2
        res = product(zq, h, 0)
        part[zq, 2 * h] = res[:, :BLOCK]
        part[zq, 2 * h + 1] = res[:, BLOCK:]
        return carry

    for xq in range(NX):
        ag_wait(slot_of(xq, yh, 1 - core), slot_of(x, yh, 1 - core))
    table_copy.wait()
    for copy in tile_copies + fetched[3:4]:
        copy.wait()
    fill(0)
    lax.fori_loop(0, EARLY, first_half, 0)
    lax.fori_loop(EARLY, BEFORE, first_half, 0)
    for k, xq in enumerate(xs):
        ag_wait(slot_of(xq, 1 - yh, core), slot_of(xq, yh, core))
        ag_send(slot_of(xq, 1 - yh, core), slot_of(x, yh, 1 - core), 12 + k)
    for o in (1, 3, 2):
        q = (ylo + o) % NYL
        feat_wait(2, q, yl_peer(q))
        feat_along(q)
    feat_wait(0, ylo, down2)
    feat_wait(4, ylo, up2)
    feat_over_y(0)
    feat_over_y(4)
    if BEFORE < 2 * NZ:
        lax.fori_loop(BEFORE, 2 * NZ, first_half, 0)
    for xq in range(NX):
        ag_wait(slot_of(xq, 1 - yh, 1 - core), slot_of(x, yh, 1 - core))
    fill(1)

    def compute(zq):
        def second_half(h, carry):
            res = product(zq, h, 1)
            part[zq, 2 * h] += res[:, :BLOCK]
            part[zq, 2 * h + 1] += res[:, BLOCK:]
            return carry

        lax.fori_loop(0, NYL // 2, second_half, 0)
    ways = (up, down)
    order = [(ylo + o) % NYL for o in (2, 1, 3, 0)]

    def chain(s):
        for yq in order:
            for d in range(2):
                dest = (z + 4 - s) % NZ if d == 0 else (z + 4 + s) % NZ
                mine = pl.ds(d * HALF, HALF)
                if s == 0:
                    zsend[d, s, yq, mine] = part[dest, yq, mine].astype(BF16)
                    src, dst = zsend.at[d, s, yq, mine], zrecv.at[d, s, yq, mine]
                elif s == 1:
                    arrived(zrecv.at[d, 0, yq, mine], z_rs.at[d, 0, yq], ways[1 - d])
                    other = pl.ds((1 - d) * HALF, HALF)
                    got = part[dest, yq, mine] + zrecv[d, 0, yq, mine].astype(F32)
                    zsend[d, s, yq, mine] = got.astype(BF16)
                    zsend[d, s, yq, other] = part[dest, yq, other].astype(BF16)
                    src, dst = zsend.at[d, s, yq], zrecv.at[d, s, yq]
                else:
                    arrived(zrecv.at[d, s - 1, yq], z_rs.at[d, s - 1, yq], ways[1 - d])
                    got = part[dest, yq] + zrecv[d, s - 1, yq].astype(F32)
                    zsend[d, s, yq] = got.astype(BF16)
                    src, dst = zsend.at[d, s, yq], zrecv.at[d, s, yq]
                start(src, dst, z_ss.at[d, s, yq], z_rs.at[d, s, yq], ways[d])

    def weight_term(lefts, rights):
        return lax.dot_general(
            jnp.concatenate(lefts, axis=1), jnp.concatenate(rights, axis=1),
            (((1,), (1,)), ((), ())), preferred_element_type=F32,
        )

    compute((z + 4) % NZ)
    chain(0)
    compute((z + 3) % NZ)
    compute((z + 5) % NZ)
    chain(1)
    for o in (2, 6, 1, 7, 0):
        compute((z + o) % NZ)
    for yq in order[::-1]:
        feat_wait(1, yq, down)
        feat_wait(3, yq, up)
    inner[...] = weight_term(
        [feats[2 + i, q] for i in (-1, 0, 1) for q in range(NYL)],
        [part[(z + NZ + i) % NZ, q].astype(BF16) for i in (-1, 0, 1) for q in range(NYL)],
    )
    chain(2)
    for yq in order[:3]:
        feat_wait(0, yq, yl_peer(yq))
        feat_wait(4, yq, yl_peer(yq))
    term = (inner[...] + weight_term(
        [feats[i, q] for i in (4, 0) for q in range(NYL)],
        [zsend[d, 2, q] for d in range(2) for q in range(NYL)],
    )).astype(BF16)
    for q in range(NG):
        w1[q, :32] = term[q * 32:(q + 1) * 32, :128]
        w1[q, 32:] = term[q * 32:(q + 1) * 32, 128:]

    def step(src_of, land, k, me, peer):
        for o in (4, 3, 5, 2, 6, 1, 7):
            q = (me + o) % 8
            start(src_of(q), land.at[me], g_ss.at[k, q], g_rs.at[k, me], peer(q))

    def take(land, k, me, peer):
        for o in (1, 7, 2, 6, 3, 5, 4):
            q = (me + o) % 8
            arrived(land.at[q], g_rs.at[k, q], peer(q))

    step(lambda q: w1.at[q], r1, 0, g, g_peer)
    r1[g] = w1[g]
    take(r1, 0, g, g_peer)
    s1[...] = jnp.sum(r1[...].astype(F32), axis=0)
    step(lambda q: s1.at[pl.ds(pl.multiple_of(q * 8, 8), 8)], r2, 1, y, y_peer)
    r2[y] = s1[pl.ds(pl.multiple_of(y * 8, 8), 8)]
    chain(3)
    take(r2, 1, y, y_peer)
    s2[...] = jnp.sum(r2[...], axis=0)
    step(lambda q: s2, r3, 2, z, z_peer)
    r3[z] = s2[...]
    for k, yq in enumerate(order):
        for d in range(2):
            arrived(zrecv.at[d, 3, yq], z_rs.at[d, 3, yq], ways[1 - d])
        total = part[z, yq] + zrecv[0, 3, yq].astype(F32) + zrecv[1, 3, yq].astype(F32)
        if k < 3:
            ysend[yq] = total.astype(BF16)
            start(ysend.at[yq], yrecv.at[ylo], y_ss.at[yq], y_rs.at[ylo], yl_peer(yq))
        else:
            own[...] = total
    take(r3, 2, z, z_peer)
    f1[y] = jnp.sum(r3[...], axis=0)
    step(lambda q: f1.at[y], f1, 3, y, y_peer)
    take(f1, 3, y, y_peer)
    f1b[...] = f1[...].reshape(64, 128).astype(BF16)
    f2[g] = f1b[...]
    step(lambda q: f1b, f2, 4, g, g_peer)

    agg = own[...]
    for yq in order[:3]:
        arrived(yrecv.at[yq], y_rs.at[yq], yl_peer(yq))
        agg = agg + yrecv[yq].astype(F32)
    gi[...] = lax.dot_general(
        agg.T.astype(BF16), wgt[...], (((1,), (1,)), ((), ())), preferred_element_type=F32
    ).astype(BF16)
    take(f2, 4, g, g_peer)
    for q in range(NG):
        gw[q * 32:(q + 1) * 32, :128] = f2[q, :32].astype(F32)
        gw[q * 32:(q + 1) * 32, 128:] = f2[q, 32:].astype(F32)
    for copy in sent:
        copy.wait_send()


def body(grad_out, relu_mask, features, weight, tile_values, tile_lists, tile_count):
    vmem = pl.BlockSpec(memory_space=pltpu.VMEM)
    dma = pltpu.SemaphoreType.DMA
    gi, gw = pl.pallas_call(
        kernel,
        out_shape=(jax.ShapeDtypeStruct((BLOCK, D), BF16), jax.ShapeDtypeStruct((D, D), F32)),
        in_specs=[pl.BlockSpec(memory_space=pl.ANY)] * 7,
        out_specs=(vmem, vmem),
        scratch_shapes=[
            pltpu.VMEM((BLOCK, D), BF16),
            pltpu.VMEM((BLOCK, D), jnp.int32),
            pltpu.VMEM((BLOCK, D), BF16),
            pltpu.VMEM((D, D), BF16),
            pltpu.VMEM((3, 1, CAP), jnp.int32),
            pltpu.SMEM((1, 1), jnp.int32),
            pltpu.VMEM((NYL, BLOCK), jnp.int32),
            pltpu.SMEM((NYL, BLOCK), jnp.int32),
            pltpu.VMEM((CAP + 1, BLOCK, BLOCK), BF16),
            pltpu.VMEM((BR, D, BLOCK), BF16),
            pltpu.VMEM((D, BR * BLOCK), BF16),
            pltpu.VMEM((NZ, NYL, D, BLOCK), F32),
            pltpu.VMEM((2, 4, NYL, D, BLOCK), BF16),
            pltpu.VMEM((2, 4, NYL, D, BLOCK), BF16),
            pltpu.VMEM((D, BLOCK), F32),
            pltpu.VMEM((NYL, D, BLOCK), BF16),
            pltpu.VMEM((NYL, D, BLOCK), BF16),
            pltpu.VMEM((5, NYL, D, BLOCK), BF16),
            pltpu.VMEM((D, D), F32),
            pltpu.VMEM((NG, 64, 128), BF16),
            pltpu.VMEM((NG, 64, 128), BF16),
            pltpu.VMEM((64, 128), F32),
            pltpu.VMEM((NY, 8, 128), F32),
            pltpu.VMEM((8, 128), F32),
            pltpu.VMEM((NZ, 8, 128), F32),
            pltpu.VMEM((NY, 8, 128), F32),
            pltpu.VMEM((64, 128), BF16),
            pltpu.VMEM((NG, 64, 128), BF16),
            dma((7,)), dma((4,)),
            dma((15,)), dma((16,)),
            dma((5, NYL)), dma((5, NYL)), dma((5, NYL)),
            dma((2, 4, NYL)), dma((2, 4, NYL)),
            dma((NYL,)), dma((NYL,)),
            dma((5, 8)), dma((5, 8)),
        ],
        compiler_params=pltpu.CompilerParams(
            collective_id=0, has_side_effects=True, vmem_limit_bytes=48 * 1024 * 1024
        ),
    )(
        *(pltpu.with_memory_space_constraint(a, pltpu.HBM) for a in (
            grad_out, relu_mask, features, weight, tile_values, tile_lists.transpose(0, 2, 1, 3)
        )),
        tile_count,
    )
    return gi[None], gw


def solution(mesh):
    return jax.shard_map(
        body,
        mesh=mesh,
        in_specs=(
            P(("row", "col"), None),
            P(("row", "col"), None),
            P("col", "row", None),
            P(),
            P("row", "col", None, None, None),
            P("row", "col", None, None),
            P("row", "col"),
        ),
        out_specs=(P("col", "row", None), P()),
        check_vma=False,
    )
```

```python
import jax
import jax.numpy as jnp
from jax import lax
from jax.experimental import pallas as pl
from jax.experimental.pallas import tpu as pltpu
from jax.sharding import PartitionSpec as P

NZ, NYL, NX, NY, NG = 8, 4, 4, 8, 8
BLOCK, D = 128, 256
BR, BC, CAP = 16, 32, 144
HALF = D // 2
EARLY, BEFORE = 2, 8
F32, BF16 = jnp.float32, jnp.bfloat16


def kernel(
    go_hbm, mask_hbm, feat_hbm, wgt_hbm, tiles, lists_hbm, count_hbm, gi, gw,
    go, mask, feat, wgt, lists, count, table_v, table, tiles_v,
    ag, dzall, part, zsend, zrecv, own, ysend, yrecv, feats, inner,
    w1, r1, s1, r2, s2, r3, f1, f1b, f2,
    in_sem, tile_sem, ag_ss, ag_rs, fy_ss, f_ss, f_rs, z_ss, z_rs,
    y_ss, y_rs, g_ss, g_rs,
):
    row, col = lax.axis_index("row"), lax.axis_index("col")
    ylo, z = row // NZ, row % NZ
    x, yh, core = col // 4, (col // 2) % 2, col % 2
    g = x * 2 + core
    y = yh * NYL + ylo

    def g_peer(q):
        return row, (q // 2) * 4 + yh * 2 + q % 2

    def y_peer(q):
        return (q % NYL) * NZ + z, x * 4 + (q // NYL) * 2 + core

    def z_peer(q):
        return ylo * NZ + q, col

    def yl_peer(q):
        return q * NZ + z, col

    def remote(src, dst, ssem, rsem, to):
        return pltpu.make_async_remote_copy(
            src_ref=src, dst_ref=dst, send_sem=ssem, recv_sem=rsem,
            device_id=to, device_id_type=pl.DeviceIdType.MESH,
        )

    sent = []

    def start(src, dst, ssem, rsem, to):
        copy = remote(src, dst, ssem, rsem, to)
        copy.start()
        sent.append(copy)

    def arrived(dst, sem, frm):
        remote(dst, dst, sem, sem, frm).wait_recv()

    barrier = pltpu.get_barrier_semaphore()
    for o in (4, 3, 5, 2, 6, 1, 7):
        for to in (y_peer((y + o) % NY), z_peer((z + o) % NZ), g_peer((g + o) % NG)):
            pl.semaphore_signal(barrier, inc=1, device_id=to, device_id_type=pl.DeviceIdType.MESH)
    fetched = []
    for i, (src, dst) in enumerate((
        (go_hbm, go), (mask_hbm, mask), (feat_hbm.at[0], feat), (wgt_hbm, wgt),
        (lists_hbm.at[0], lists), (count_hbm, count),
    )):
        copy = pltpu.make_async_copy(src, dst, in_sem.at[i])
        copy.start()
        fetched.append(copy)
    tile_copies = []
    for i in range(4):
        part_of = pl.ds(i * (CAP // 4), CAP // 4)
        copy = pltpu.make_async_copy(tiles.at[0, 0, part_of], tiles_v.at[part_of], tile_sem.at[i])
        copy.start()
        tile_copies.append(copy)
    fetched[0].wait()
    fetched[1].wait()
    dz = go[...].astype(F32) * mask[...].astype(F32)
    ag[col] = dz.T.astype(BF16)
    fetched[2].wait()
    feats[2, ylo] = feat[...].astype(F32).T.astype(BF16)
    fetched[4].wait()
    fetched[5].wait()
    tiles_v[CAP] = jnp.zeros((BLOCK, BLOCK), BF16)
    place = (lists[1] - col * BC) * BR + lists[0] - row * BR
    live = lax.broadcasted_iota(jnp.int32, (1, CAP), 1) < count[0, 0]
    place = jnp.broadcast_to(jnp.where(live, place, -1), (BLOCK, CAP)).T
    slots = jnp.broadcast_to(lists[2], (BLOCK, CAP)).T
    lane = lax.broadcasted_iota(jnp.int32, (CAP, BLOCK), 1)
    for b in range(NYL):
        table_v[b:b + 1] = jnp.min(
            jnp.where(place == lane + b * BLOCK, slots, CAP), axis=0, keepdims=True
        )
    table_copy = pltpu.make_async_copy(table_v, table, in_sem.at[6])
    table_copy.start()
    pl.semaphore_wait(barrier, 21)

    def slot_of(xq, yq, cq):
        return xq * 4 + yq * 2 + cq

    def ag_send(slot, to_col, k):
        start(ag.at[slot], ag.at[slot], ag_ss.at[k], ag_rs.at[slot], (row, to_col))

    def ag_wait(slot, from_col):
        arrived(ag.at[slot], ag_rs.at[slot], (row, from_col))

    xs = [(x + o) % NX for o in (2, 1, 3)]
    over = slot_of(x, 1 - yh, core)
    ag_send(col, over, 0)
    for k, xq in enumerate(xs):
        ag_send(col, slot_of(xq, yh, core), 1 + k)
    ag_send(col, slot_of(x, yh, 1 - core), 4)
    up, down = z_peer((z + 1) % NZ), z_peer((z + NZ - 1) % NZ)
    up2, down2 = z_peer((z + 2) % NZ), z_peer((z + NZ - 2) % NZ)
    for dst, to in ((0, up2), (4, down2)):
        start(feats.at[2, ylo], feats.at[dst, ylo], f_ss.at[dst, ylo], f_rs.at[dst, ylo], to)

    def feat_over_y(at):
        for o in (2, 1, 3):
            q = (ylo + o) % NYL
            start(feats.at[at, ylo], feats.at[at, ylo], fy_ss.at[at, q], f_rs.at[at, ylo], yl_peer(q))

    feat_over_y(2)

    def feat_along(yq):
        for dst, to in ((1, up), (3, down)):
            start(feats.at[2, yq], feats.at[dst, yq], f_ss.at[dst, yq], f_rs.at[dst, yq], to)

    def feat_wait(at, yq, frm):
        arrived(feats.at[at, yq], f_rs.at[at, yq], frm)

    ag_wait(over, over)
    for k, xq in enumerate(xs):
        ag_send(over, slot_of(xq, yh, core), 5 + k)
    ag_send(over, slot_of(x, yh, 1 - core), 8)
    for k, xq in enumerate(xs):
        ag_wait(slot_of(xq, yh, core), slot_of(xq, yh, core))
        ag_send(slot_of(xq, yh, core), slot_of(x, yh, 1 - core), 9 + k)

    feat_along(ylo)

    sides = (yh, 1 - yh)

    def fill(side):
        for k in range(8):
            at = (side * 8 + k) * BLOCK
            dzall[:, at:at + BLOCK] = ag[slot_of(k // 2, sides[side], k % 2)]

    def product(zq, h, side):
        first = zq * BR + sides[side] * 2
        rhs = jnp.concatenate([
            jnp.concatenate(
                [tiles_v[table[2 * h + j, first + (k // 2) * 4 + k % 2]] for k in range(8)], axis=0
            )
            for j in range(2)
        ], axis=1)
        lhs = dzall[:, side * 8 * BLOCK:(side + 1) * 8 * BLOCK]
        return jnp.dot(lhs, rhs, preferred_element_type=F32)

    def first_half(t, carry):
        zq, h = t // 2, t % 2
        res = product(zq, h, 0)
        part[zq, 2 * h] = res[:, :BLOCK]
        part[zq, 2 * h + 1] = res[:, BLOCK:]
        return carry

    for xq in range(NX):
        ag_wait(slot_of(xq, yh, 1 - core), slot_of(x, yh, 1 - core))
    table_copy.wait()
    for copy in tile_copies + fetched[3:4]:
        copy.wait()
    fill(0)
    lax.fori_loop(0, EARLY, first_half, 0)
    lax.fori_loop(EARLY, BEFORE, first_half, 0)
    for k, xq in enumerate(xs):
        ag_wait(slot_of(xq, 1 - yh, core), slot_of(xq, yh, core))
        ag_send(slot_of(xq, 1 - yh, core), slot_of(x, yh, 1 - core), 12 + k)
    for o in (1, 3, 2):
        q = (ylo + o) % NYL
        feat_wait(2, q, yl_peer(q))
        feat_along(q)
    feat_wait(0, ylo, down2)
    feat_wait(4, ylo, up2)
    feat_over_y(0)
    feat_over_y(4)
    if BEFORE < 2 * NZ:
        lax.fori_loop(BEFORE, 2 * NZ, first_half, 0)
    for xq in range(NX):
        ag_wait(slot_of(xq, 1 - yh, 1 - core), slot_of(x, yh, 1 - core))
    fill(1)

    def compute(zq):
        def second_half(h, carry):
            res = product(zq, h, 1)
            part[zq, 2 * h] += res[:, :BLOCK]
            part[zq, 2 * h + 1] += res[:, BLOCK:]
            return carry

        lax.fori_loop(0, NYL // 2, second_half, 0)
    ways = (up, down)
    order = [(ylo + o) % NYL for o in (2, 1, 3, 0)]

    def chain(s):
        for yq in order:
            for d in range(2):
                dest = (z + 4 - s) % NZ if d == 0 else (z + 4 + s) % NZ
                mine = pl.ds(d * HALF, HALF)
                if s == 0:
                    zsend[d, s, yq, mine] = part[dest, yq, mine].astype(BF16)
                    src, dst = zsend.at[d, s, yq, mine], zrecv.at[d, s, yq, mine]
                elif s == 1:
                    arrived(zrecv.at[d, 0, yq, mine], z_rs.at[d, 0, yq], ways[1 - d])
                    other = pl.ds((1 - d) * HALF, HALF)
                    got = part[dest, yq, mine] + zrecv[d, 0, yq, mine].astype(F32)
                    zsend[d, s, yq, mine] = got.astype(BF16)
                    zsend[d, s, yq, other] = part[dest, yq, other].astype(BF16)
                    src, dst = zsend.at[d, s, yq], zrecv.at[d, s, yq]
                else:
                    arrived(zrecv.at[d, s - 1, yq], z_rs.at[d, s - 1, yq], ways[1 - d])
                    got = part[dest, yq] + zrecv[d, s - 1, yq].astype(F32)
                    zsend[d, s, yq] = got.astype(BF16)
                    src, dst = zsend.at[d, s, yq], zrecv.at[d, s, yq]
                start(src, dst, z_ss.at[d, s, yq], z_rs.at[d, s, yq], ways[d])

    def weight_term(lefts, rights):
        return lax.dot_general(
            jnp.concatenate(lefts, axis=1), jnp.concatenate(rights, axis=1),
            (((1,), (1,)), ((), ())), preferred_element_type=F32,
        )

    compute((z + 4) % NZ)
    chain(0)
    compute((z + 3) % NZ)
    compute((z + 5) % NZ)
    compute((z + 2) % NZ)
    compute((z + 6) % NZ)
    chain(1)
    for o in (1, 7, 0):
        compute((z + o) % NZ)
    for yq in order[::-1]:
        feat_wait(1, yq, down)
        feat_wait(3, yq, up)
    inner[...] = weight_term(
        [feats[2 + i, q] for i in (-1, 0, 1) for q in range(NYL)],
        [part[(z + NZ + i) % NZ, q].astype(BF16) for i in (-1, 0, 1) for q in range(NYL)],
    )
    chain(2)
    for yq in order[:3]:
        feat_wait(0, yq, yl_peer(yq))
        feat_wait(4, yq, yl_peer(yq))
    term = (inner[...] + weight_term(
        [feats[i, q] for i in (4, 0) for q in range(NYL)],
        [zsend[d, 2, q] for d in range(2) for q in range(NYL)],
    )).astype(BF16)
    for q in range(NG):
        w1[q, :32] = term[q * 32:(q + 1) * 32, :128]
        w1[q, 32:] = term[q * 32:(q + 1) * 32, 128:]

    def step(src_of, land, k, me, peer):
        for o in (4, 3, 5, 2, 6, 1, 7):
            q = (me + o) % 8
            start(src_of(q), land.at[me], g_ss.at[k, q], g_rs.at[k, me], peer(q))

    def take(land, k, me, peer):
        for o in (1, 7, 2, 6, 3, 5, 4):
            q = (me + o) % 8
            arrived(land.at[q], g_rs.at[k, q], peer(q))

    step(lambda q: w1.at[q], r1, 0, g, g_peer)
    r1[g] = w1[g]
    take(r1, 0, g, g_peer)
    s1[...] = jnp.sum(r1[...].astype(F32), axis=0)
    step(lambda q: s1.at[pl.ds(pl.multiple_of(q * 8, 8), 8)], r2, 1, y, y_peer)
    r2[y] = s1[pl.ds(pl.multiple_of(y * 8, 8), 8)]
    chain(3)
    take(r2, 1, y, y_peer)
    s2[...] = jnp.sum(r2[...], axis=0)
    step(lambda q: s2, r3, 2, z, z_peer)
    r3[z] = s2[...]
    for k, yq in enumerate(order):
        for d in range(2):
            arrived(zrecv.at[d, 3, yq], z_rs.at[d, 3, yq], ways[1 - d])
        total = part[z, yq] + zrecv[0, 3, yq].astype(F32) + zrecv[1, 3, yq].astype(F32)
        if k < 3:
            ysend[yq] = total.astype(BF16)
            start(ysend.at[yq], yrecv.at[ylo], y_ss.at[yq], y_rs.at[ylo], yl_peer(yq))
        else:
            own[...] = total
    take(r3, 2, z, z_peer)
    f1[y] = jnp.sum(r3[...], axis=0)
    step(lambda q: f1.at[y], f1, 3, y, y_peer)
    take(f1, 3, y, y_peer)
    f1b[...] = f1[...].reshape(64, 128).astype(BF16)
    f2[g] = f1b[...]
    step(lambda q: f1b, f2, 4, g, g_peer)

    agg = own[...]
    for yq in order[:3]:
        arrived(yrecv.at[yq], y_rs.at[yq], yl_peer(yq))
        agg = agg + yrecv[yq].astype(F32)
    gi[...] = lax.dot_general(
        agg.T.astype(BF16), wgt[...], (((1,), (1,)), ((), ())), preferred_element_type=F32
    ).astype(BF16)
    take(f2, 4, g, g_peer)
    for q in range(NG):
        gw[q * 32:(q + 1) * 32, :128] = f2[q, :32].astype(F32)
        gw[q * 32:(q + 1) * 32, 128:] = f2[q, 32:].astype(F32)
    for copy in sent:
        copy.wait_send()


def body(grad_out, relu_mask, features, weight, tile_values, tile_lists, tile_count):
    vmem = pl.BlockSpec(memory_space=pltpu.VMEM)
    dma = pltpu.SemaphoreType.DMA
    gi, gw = pl.pallas_call(
        kernel,
        out_shape=(jax.ShapeDtypeStruct((BLOCK, D), BF16), jax.ShapeDtypeStruct((D, D), F32)),
        in_specs=[pl.BlockSpec(memory_space=pl.ANY)] * 7,
        out_specs=(vmem, vmem),
        scratch_shapes=[
            pltpu.VMEM((BLOCK, D), BF16),
            pltpu.VMEM((BLOCK, D), jnp.int32),
            pltpu.VMEM((BLOCK, D), BF16),
            pltpu.VMEM((D, D), BF16),
            pltpu.VMEM((3, 1, CAP), jnp.int32),
            pltpu.SMEM((1, 1), jnp.int32),
            pltpu.VMEM((NYL, BLOCK), jnp.int32),
            pltpu.SMEM((NYL, BLOCK), jnp.int32),
            pltpu.VMEM((CAP + 1, BLOCK, BLOCK), BF16),
            pltpu.VMEM((BR, D, BLOCK), BF16),
            pltpu.VMEM((D, BR * BLOCK), BF16),
            pltpu.VMEM((NZ, NYL, D, BLOCK), F32),
            pltpu.VMEM((2, 4, NYL, D, BLOCK), BF16),
            pltpu.VMEM((2, 4, NYL, D, BLOCK), BF16),
            pltpu.VMEM((D, BLOCK), F32),
            pltpu.VMEM((NYL, D, BLOCK), BF16),
            pltpu.VMEM((NYL, D, BLOCK), BF16),
            pltpu.VMEM((5, NYL, D, BLOCK), BF16),
            pltpu.VMEM((D, D), F32),
            pltpu.VMEM((NG, 64, 128), BF16),
            pltpu.VMEM((NG, 64, 128), BF16),
            pltpu.VMEM((64, 128), F32),
            pltpu.VMEM((NY, 8, 128), F32),
            pltpu.VMEM((8, 128), F32),
            pltpu.VMEM((NZ, 8, 128), F32),
            pltpu.VMEM((NY, 8, 128), F32),
            pltpu.VMEM((64, 128), BF16),
            pltpu.VMEM((NG, 64, 128), BF16),
            dma((7,)), dma((4,)),
            dma((15,)), dma((16,)),
            dma((5, NYL)), dma((5, NYL)), dma((5, NYL)),
            dma((2, 4, NYL)), dma((2, 4, NYL)),
            dma((NYL,)), dma((NYL,)),
            dma((5, 8)), dma((5, 8)),
        ],
        compiler_params=pltpu.CompilerParams(
            collective_id=0, has_side_effects=True, vmem_limit_bytes=48 * 1024 * 1024
        ),
    )(
        *(pltpu.with_memory_space_constraint(a, pltpu.HBM) for a in (
            grad_out, relu_mask, features, weight, tile_values, tile_lists.transpose(0, 2, 1, 3)
        )),
        tile_count,
    )
    return gi[None], gw


def solution(mesh):
    return jax.shard_map(
        body,
        mesh=mesh,
        in_specs=(
            P(("row", "col"), None),
            P(("row", "col"), None),
            P("col", "row", None),
            P(),
            P("row", "col", None, None, None),
            P("row", "col", None, None),
            P("row", "col"),
        ),
        out_specs=(P("col", "row", None), P()),
        check_vma=False,
    )
```
